32 devices in a mesh: exp: 8 (over z, core), ccd: 4 (over y, x).
Axes of the slice: x: 2, y: 2, z: 4, core: 2. Of those that a mesh axis runs over, the one named last changes fastest.
Arguments:
- pixels: bfloat16 [8, 4000, 4, 128], P('exp', 'ccd'), may hold values from -24 to 24
- psf_proj: bfloat16 [8, 100, 2160], P('ccd'), may hold values from -0.5 to 0.5
- resolution: float32 [200, 11, 512], P('ccd', None, 'exp'), may hold values from 0.02 to 0.16
- basis: float32 [10, 528], replicated, may hold values from -4 to 4
- sky_fibres: int32 [24], replicated, may hold values from 0 to 199, as said below
- fibre_slot: int32 [200], P('ccd'), may hold values from 0 to 199, as said below
- band_shift: int32 [200], P('ccd'), may hold values from -3 to 3
Outputs:
- sky_subtracted: float32 [8, 200, 512], P(None, 'ccd', 'exp')
- noise_rms: float32 [200, 512], P('ccd', 'exp')
The draws below stay inside these ranges and needn't reach their ends.
Inputs may be any that keep to these rules, and one draw needn't show every extreme that they name: `sky_fibres`: 24 distinct fibre numbers, listed group by group: entries g * 6 to (g + 1) * 6 - 1 are fibres of the group g of 50 consecutive fibres. `fibre_slot`: for each group g of 50 consecutive fibres, a permutation of the slots g * 50 to (g + 1) * 50 - 1.
All inputs are finite; a program needn't handle non-finite values.
Results may differ from the reference program's by a relative error of at most 0.00095.
Values may be sent and summed in bfloat16 or wider, within the bound.
A program may use at most 64 MiB of HBM per device.

```python
import jax
import jax.numpy as jnp
from jax import lax

FIBBLK = 25
BPIX = 500
MARG = 20
ROWS = 4
COMP = 10
BAND = 11
SHIFT = 3
WAVE = 512
EXPOS = 8
NBLK = 8
COLS = 4000
FIB = 200
FC = 50
GROUPS = 128
SPAN = 540
EXT = 528
SKYC = 6
SKY = 24


def sky_parts(key):
    inner = jax.random.fold_in(key, 17)
    first, second = jax.random.split(inner)
    spectra = jnp.clip(jax.random.normal(first, (COMP, EXT), jnp.float32), -4.0, 4.0)
    weights = jnp.clip(0.6 * jax.random.normal(second, (EXPOS, COMP), jnp.float32), -1.8, 1.8)
    return (spectra, weights)


def draw_basis(key, part):
    return sky_parts(key)[0]


def draw_pixels(key, part):
    spectra, weights = sky_parts(key)
    centre = spectra[:, SHIFT + BAND // 2:SHIFT + BAND // 2 + WAVE]
    glow = jnp.sum(weights[:, :, None] * centre[None, :, :], axis=1)
    glow = glow.reshape(EXPOS, ROWS, GROUPS)[:, None, :, :]
    noise = jnp.clip(jax.random.normal(jax.random.fold_in(key, 29), (EXPOS, COLS, ROWS, GROUPS), jnp.float32), -5.0, 5.0)
    return jnp.clip(noise + glow, -24.0, 24.0).astype(jnp.bfloat16)


def draw_psf_proj(key, part):
    inner = jax.random.fold_in(key, 41)
    spread = jnp.clip(jax.random.normal(inner, (NBLK, FIBBLK * ROWS, SPAN * ROWS), jnp.float32), -5.0, 5.0)
    spread = spread / float(SPAN * ROWS) ** 0.5
    out_row = jnp.arange(FIBBLK * ROWS, dtype=jnp.int32) % ROWS
    in_row = jnp.arange(SPAN * ROWS, dtype=jnp.int32) % ROWS
    level = jnp.where(out_row[:, None] == in_row[None, :], 1.0 / SPAN, 0.0).astype(jnp.float32)
    return (spread + level[None, :, :]).astype(jnp.bfloat16)


def draw_sky_fibres(key, part):
    inner = jax.random.fold_in(key, 53)
    count = FIB // FC
    keys = jax.random.split(inner, count)
    orders = jax.vmap(lambda single: jax.random.permutation(single, FC)[:SKYC])(keys).astype(jnp.int32)
    starts = (jnp.arange(count, dtype=jnp.int32) * FC)[:, None]
    return (orders + starts).reshape(SKY)


def draw_fibre_slot(key, part):
    inner = jax.random.fold_in(key, 67)
    count = FIB // FC
    keys = jax.random.split(inner, count)
    orders = jax.vmap(lambda single: jax.random.permutation(single, FC))(keys).astype(jnp.int32)
    starts = (jnp.arange(count, dtype=jnp.int32) * FC)[:, None]
    return (orders + starts).reshape(FIB)


def set_ends(entries, rng, low, top_value):
    longest = entries.shape.index(max(entries.shape))
    spots = []
    for shift in (0, 1):
        where = [jax.random.randint(jax.random.fold_in(rng, axis), (), 0, length) for axis, length in enumerate(entries.shape)]
        where[longest] = (where[longest] + shift) % entries.shape[longest]
        spots.append(tuple(where))
    return entries.at[spots[0]].set(low).at[spots[1]].set(top_value)


def shard_levels(rng, shape, cuts, least, high):
    level, own = 1.0, jax.random.fold_in(rng, 6)
    for axis_at, parts in cuts:
        steps = jnp.exp(jax.random.uniform(jax.random.fold_in(own, axis_at), (parts,), jnp.float32, least / len(cuts), high / len(cuts)))
        level = level * jnp.repeat(steps, shape[axis_at] // parts).reshape([-1 if axis == axis_at else 1 for axis in range(len(shape))])
    return level


def setup_inputs(seed: int = 0) -> dict:
    key_of = jax.random.split(jax.random.key(seed), 8)
    pixels = draw_pixels(jax.random.fold_in(key_of[7], 71), 0)
    psf_proj = draw_psf_proj(jax.random.fold_in(key_of[7], 71), 0)
    resolution = jnp.clip(0.02 + 0.14 * jax.random.uniform(key_of[2], (FIB, BAND, WAVE), jnp.float32) ** shard_levels(key_of[2], (FIB, BAND, WAVE), ((0, 4), (2, 8)), -0.2, 0.2), 0.02, 0.16)
    basis = draw_basis(jax.random.fold_in(key_of[7], 71), 0)
    sky_fibres = draw_sky_fibres(jax.random.fold_in(key_of[7], 71), 0)
    fibre_slot = draw_fibre_slot(jax.random.fold_in(key_of[7], 71), 0)
    band_shift = set_ends(jax.random.randint(key_of[6], (FIB,), 0 - SHIFT, SHIFT + 1), jax.random.fold_in(key_of[6], 1), 0 - SHIFT, SHIFT).astype(jnp.int32)
    return dict(pixels=pixels, psf_proj=psf_proj, resolution=resolution, basis=basis, sky_fibres=sky_fibres, fibre_slot=fibre_slot, band_shift=band_shift)


def band_model(pieces, spectra, shifts, first):
    length = pieces.shape[2]

    def window_of(shift):
        return lax.dynamic_slice(spectra, (jnp.int32(0), (first + shift + SHIFT).astype(jnp.int32)), (spectra.shape[0], length + BAND - 1))
    windows = jax.vmap(window_of)(shifts)
    total = jnp.zeros((pieces.shape[0], spectra.shape[0], length), jnp.float32)
    for offset in range(BAND):
        total = total + pieces[:, offset, None, :] * windows[:, :, offset:offset + length]
    return total

def solve_small(gram, target):
    factor = jnp.linalg.cholesky(gram)
    return jax.scipy.linalg.cho_solve((factor, True), target[..., None])[..., 0]

def reference(pixels, psf_proj, resolution, basis, sky_fibres, fibre_slot, band_shift):
    exposures = pixels.shape[0]
    padded = jnp.pad(pixels, ((0, 0), (MARG, MARG), (0, 0), (0, 0)))
    proj_square = jnp.square(psf_proj.astype(jnp.float32)).astype(jnp.bfloat16)
    proj_square = lax.optimization_barrier(proj_square)

    def extract(block):
        window = lax.dynamic_slice_in_dim(padded, block * BPIX, SPAN, 1).astype(jnp.float32)
        pixvar = (0.25 + jnp.square(window)).astype(jnp.bfloat16)
        pixvar = lax.optimization_barrier(pixvar).astype(jnp.float32)
        window = window.reshape(exposures, SPAN * ROWS, GROUPS)
        pixvar = pixvar.reshape(exposures, SPAN * ROWS, GROUPS)
        weights = lax.dynamic_index_in_dim(psf_proj, block, 0, keepdims=False).astype(jnp.float32)
        squares = lax.dynamic_index_in_dim(proj_square, block, 0, keepdims=False).astype(jnp.float32)
        flux_block = jnp.einsum('oi,eig->eog', weights, window)
        var_block = jnp.einsum('oi,eig->eog', squares, pixvar)
        return (flux_block, var_block)
    flux_blocks, var_blocks = lax.map(extract, jnp.arange(NBLK, dtype=jnp.int32))

    def arrange(blocks):
        ordered = blocks.reshape(NBLK, exposures, FIBBLK, ROWS, GROUPS).transpose(1, 0, 2, 3, 4)
        return ordered.reshape(exposures, FIB, WAVE)[:, fibre_slot, :]
    flux = arrange(flux_blocks)
    variance = arrange(var_blocks)
    model = band_model(resolution, basis, band_shift, 0)
    skymask = jnp.any(jnp.arange(FIB, dtype=jnp.int32)[:, None] == sky_fibres[None, :], axis=1).astype(jnp.float32)
    highest = lax.Precision.HIGHEST

    def normal_eqs(pair):
        flux_one, var_one = pair
        weight = skymask[:, None] / var_one
        weighted = model * weight[:, None, :]
        gram = jnp.einsum('fkw,flw->kl', weighted, model, precision=highest)
        target = jnp.einsum('fkw,fw->k', weighted, flux_one, precision=highest)
        return (gram, target)
    grams, targets = lax.map(normal_eqs, (flux, variance))
    coeffs = solve_small(grams, targets)

    def subtract(pair):
        flux_one, coeff_one = pair
        return flux_one - jnp.einsum('k,fkw->fw', coeff_one, model, precision=highest)
    sky_subtracted = lax.map(subtract, (flux, coeffs))
    centred = sky_subtracted - lax.optimization_barrier(jnp.mean(sky_subtracted, axis=0))
    noise_rms = jnp.sqrt(lax.optimization_barrier(jnp.mean(jnp.square(centred), axis=0)) + 1e-06)
    return (sky_subtracted, noise_rms)
```

```python
import functools

import jax
import jax.numpy as jnp
from jax import lax
from jax.experimental import pallas as pl
from jax.experimental.pallas import tpu as pltpu
from jax.sharding import PartitionSpec as P

BPIX = 500
MARG = 20
ROWS = 4
BAND = 11
SHIFT = 3
SPAN = 540
LANES = 128
TAPS = BAND + 2 * SHIFT
HALO = MARG * ROWS
DEEP = SPAN * ROWS
SLOTS = 64
SKYROW = 56
MESH = pl.DeviceIdType.MESH


def column_of(row, count):
    n = row.shape[1]
    sub = lax.broadcasted_iota(jnp.int32, (count, n), 0)
    lane = lax.broadcasted_iota(jnp.int32, (count, n), 1)
    return jnp.sum(jnp.where(sub == lane, row, 0), axis=1, keepdims=True)


def pieces_of(x):
    high = x.astype(jnp.bfloat16)
    rest = x - high.astype(jnp.float32)
    mid = rest.astype(jnp.bfloat16)
    low = (rest - mid.astype(jnp.float32)).astype(jnp.bfloat16)
    return high, mid, low


def kernel(
    n_e, n_c, skyc, comp,
    pix_hbm, psf_hbm, res_hbm, basis_ref, slot_row, shift_row, sky_s, slot_s, shift_s,
    out_ref, rms_ref,
    xs, psf, res, res2, bpad, bsh, stage, skysend, skyrecv, skyfull, slots, fluxr,
    fsend, frecv, grecv, csend, crecv, croll, outs,
    local_sem, halo_ssem, halo_rsem, sky_ssem, sky_rsem, f_ssem, f_rsem,
    g_ssem, g_rsem, c_ssem, c_rsem,
):
    me = lax.axis_index("exp")
    mc = lax.axis_index("ccd")
    fc = res.shape[1]
    wl = res.shape[2]
    own = pix_hbm.shape[0]
    groups = LANES // wl
    tall = SLOTS // groups
    per = stage.shape[0]
    half = psf.shape[1]
    f32 = jnp.float32

    get_res = pltpu.make_async_copy(res_hbm, res, local_sem.at[0])
    get_psf = pltpu.make_async_copy(psf_hbm, psf, local_sem.at[1])
    get_pix = pltpu.make_async_copy(pix_hbm, xs.at[pl.ds(HALO, own)], local_sem.at[2])
    get_res.start()
    get_psf.start()
    get_pix.start()

    barrier = pltpu.get_barrier_semaphore()
    for d in range(1, n_e):
        pl.semaphore_signal(
            barrier, inc=1, device_id={"exp": lax.rem(me + d, n_e)}, device_id_type=MESH
        )
    for d in range(1, n_c):
        pl.semaphore_signal(
            barrier, inc=1, device_id={"ccd": lax.rem(mc + d, n_c)}, device_id_type=MESH
        )

    sky = [jnp.clip(sky_s[mc * skyc + i] - mc * fc, 0, fc - 1) for i in range(skyc)]

    stage[...] = jnp.zeros_like(stage)
    bpad[...] = jnp.zeros_like(bpad)
    bpad[0:comp, 0 : basis_ref.shape[1]] = basis_ref[...]
    get_res.wait()
    for i in range(skyc):
        q, s = i // per, i % per
        for d in range(BAND):
            stage[s, d : d + 1, q * wl : (q + 1) * wl] = res[d, pl.ds(sky[i], 1), :]
    skysend[...] = stage[...].astype(jnp.bfloat16)

    pl.semaphore_wait(barrier, n_e - 1 + n_c - 1)

    def to_left():
        return pltpu.make_async_remote_copy(
            src_ref=pix_hbm.at[pl.ds(0, HALO)],
            dst_ref=xs.at[pl.ds(HALO + own, HALO)],
            send_sem=halo_ssem.at[0],
            recv_sem=halo_rsem.at[0],
            device_id={"ccd": lax.rem(mc + n_c - 1, n_c)},
            device_id_type=MESH,
        )

    def to_right():
        return pltpu.make_async_remote_copy(
            src_ref=pix_hbm.at[pl.ds(own - HALO, HALO)],
            dst_ref=xs.at[pl.ds(0, HALO)],
            send_sem=halo_ssem.at[1],
            recv_sem=halo_rsem.at[1],
            device_id={"ccd": lax.rem(mc + 1, n_c)},
            device_id_type=MESH,
        )

    @pl.when(mc > 0)
    def _():
        to_left().start()

    @pl.when(mc < n_c - 1)
    def _():
        to_right().start()

    @pl.when(mc == 0)
    def _():
        xs[0:HALO, :] = jnp.zeros((HALO, LANES), xs.dtype)

    @pl.when(mc == n_c - 1)
    def _():
        xs[HALO + own :, :] = jnp.zeros((HALO, LANES), xs.dtype)

    def exchange(axis, size, mine, source, landing, ssem, rsem):
        sends, receives = [], []
        for d in range(1, size):
            there = lax.rem(mine + d, size)
            origin = lax.rem(mine + size - d, size)
            sends.append(
                pltpu.make_async_remote_copy(
                    src_ref=source(there), dst_ref=landing.at[mine],
                    send_sem=ssem.at[d], recv_sem=rsem.at[mine],
                    device_id={axis: there}, device_id_type=MESH,
                )
            )
            receives.append(
                pltpu.make_async_remote_copy(
                    src_ref=source(there), dst_ref=landing.at[origin],
                    send_sem=ssem.at[d], recv_sem=rsem.at[origin],
                    device_id={axis: there}, device_id_type=MESH,
                )
            )
        return sends, receives

    sky_out, sky_in = exchange(
        "exp", n_e, me, lambda there: skysend, skyrecv, sky_ssem, sky_rsem
    )
    for copy in sky_out:
        copy.start()
    skyrecv[me] = skysend[...]

    wide = bsh.shape[2]
    for e in range(TAPS):
        bsh[e] = bpad[:, e : e + wide]

    slot = column_of(slot_row[...], SLOTS) - mc * fc
    place = lax.broadcasted_iota(jnp.int32, (SLOTS, 1), 0)
    slot = jnp.where(place < fc, slot, -1000)
    for i in range(skyc):
        slot = jnp.where(place == SKYROW + i, slot_s[sky[i]] - mc * fc, slot)
    gap = slots.shape[0] // 2 - half
    first = slot * ROWS + jnp.where(slot * ROWS >= half, gap, 0)
    lane = lax.broadcasted_iota(jnp.int32, (SLOTS, slots.shape[0]), 1)
    pick = jnp.concatenate(
        [jnp.where(lane == first + r, 1.0, 0.0) for r in range(ROWS)], axis=0
    ).astype(jnp.bfloat16)

    slots[...] = jnp.zeros_like(slots)
    get_psf.wait()
    get_pix.wait()

    def partial(block, lower, upper):
        weights = psf[block, :, lower:upper]
        start = block * BPIX * ROWS
        window = xs[start + lower : start + upper, :]
        wide_w = weights.astype(f32)
        wide_x = window.astype(f32)
        squares = (wide_w * wide_w).astype(jnp.bfloat16)
        pixvar = (0.25 + wide_x * wide_x).astype(jnp.bfloat16)
        flux = jnp.dot(weights, window, preferred_element_type=f32)
        var = jnp.dot(squares, pixvar, preferred_element_type=f32)
        return flux, var

    blocks = psf.shape[0]
    cuts = []
    for b in range(blocks):
        lower = LANES if b == 0 else 0
        upper = (DEEP - HALO) // LANES * LANES if b == blocks - 1 else DEEP
        cuts.append((lower, upper))
    main = [partial(b, *cuts[b]) for b in range(blocks)]

    @pl.when(mc < n_c - 1)
    def _():
        to_left().wait_recv()

    @pl.when(mc > 0)
    def _():
        to_right().wait_recv()

    pitch = slots.shape[0] // 2
    for b in range(blocks):
        flux, var = main[b]
        lower, upper = cuts[b]
        if lower > 0:
            more = partial(b, 0, lower)
            flux, var = flux + more[0], var + more[1]
        if upper < DEEP:
            more = partial(b, upper, DEEP)
            flux, var = flux + more[0], var + more[1]
        slots[b * pitch : b * pitch + half, 0:LANES] = flux
        slots[b * pitch : b * pitch + half, LANES:] = var

    high, mid, low = pieces_of(slots[...])
    dot = functools.partial(jnp.dot, preferred_element_type=f32)
    chosen = dot(pick, high) + (dot(pick, mid) + dot(pick, low))
    fluxr[...] = chosen

    for j in range(n_e):
        r, off = j * wl // LANES, j * wl % LANES
        for q in range(groups):
            rows = pl.ds(r * SLOTS + q * tall, tall)
            fsend[j, :, q * wl : (q + 1) * wl] = fluxr[rows, off : off + wl]
    f_out, f_in = exchange(
        "exp", n_e, me, lambda there: fsend.at[there], frecv, f_ssem, f_rsem
    )
    for copy in f_out:
        copy.start()
    frecv[me] = fsend[me]

    for copy in sky_in:
        copy.wait_recv()
    for j in range(n_e):
        block = skyrecv[j].astype(f32)
        for i in range(skyc):
            q, s = i // per, i % per
            skyfull[i, :, j * wl : (j + 1) * wl] = block[s, :, q * wl : (q + 1) * wl]
    sub = lax.broadcasted_iota(jnp.int32, (16, wide), 0)
    sums = [jnp.zeros((16, LANES), f32) for _ in range(comp + 1)]
    for i in range(skyc):
        offset = jnp.clip(shift_s[sky[i]] + SHIFT, 0, 2 * SHIFT)
        model = jnp.zeros((16, wide), f32)
        for d in range(BAND):
            model = model + skyfull[i, d : d + 1, :] * bsh[offset + d]
        rows = [r * SLOTS + SKYROW + i for r in range(ROWS)]
        flux = jnp.concatenate([fluxr[x : x + 1, 0:LANES] for x in rows], axis=1)
        var = jnp.concatenate([fluxr[x : x + 1, LANES:] for x in rows], axis=1)
        full = jnp.where(sub == comp, flux, model)
        weighted = full * (1.0 / var)
        for col in range(comp + 1):
            product = weighted * full[col : col + 1, :]
            for t in range(0, wide, LANES):
                sums[col] = sums[col] + product[:, t : t + LANES]
    lanes16 = lax.broadcasted_iota(jnp.int32, (16, LANES), 1)
    sub16 = lax.broadcasted_iota(jnp.int32, (16, LANES), 0)
    gram = jnp.zeros((16, LANES), f32)
    for col in range(comp + 1):
        gram = jnp.where(lanes16 == col, jnp.sum(sums[col], axis=1, keepdims=True), gram)
    grecv[mc] = gram
    g_out, g_in = exchange(
        "ccd", n_c, mc, lambda there: grecv.at[mc], grecv, g_ssem, g_rsem
    )
    for copy in g_out:
        copy.start()

    planes = [res[d] for d in range(BAND)]
    shift = column_of(shift_row[...], fc) + SHIFT
    for step in (1, 2, 4):
        take = jnp.bitwise_and(shift, step) != 0
        length = min(len(planes) + step, TAPS)
        moved = []
        for e in range(length):
            here = planes[e] if e < len(planes) else jnp.zeros((fc, wl), f32)
            before = planes[e - step] if e >= step else jnp.zeros((fc, wl), f32)
            moved.append(jnp.where(take, before, here))
        planes = moved
    for e in range(TAPS):
        res2[e] = planes[e]

    for copy in g_in:
        copy.wait_recv()
    m = grecv[0]
    for c in range(1, n_c):
        m = m + grecv[c]
    for k in range(comp):
        row = m[k : k + 1, :] / m[k : k + 1, k : k + 1]
        m = jnp.where(sub16 == k, row, m - m[:, k : k + 1] * row)
    coeffs = jnp.where(sub16[:, 0:1] < comp, m[:, comp : comp + 1], 0.0)
    spectrum = jnp.sum(coeffs * bpad[...], axis=0, keepdims=True)
    for j in range(n_e):
        csend[j] = spectrum[:, j * wl : j * wl + LANES]
    c_out, c_in = exchange(
        "exp", n_e, me, lambda there: csend.at[there], crecv, c_ssem, c_rsem
    )
    for copy in c_out:
        copy.start()
    crecv[me] = csend[me]
    for copy in f_in:
        copy.wait_recv()
    for copy in c_in:
        copy.wait_recv()

    fitted = jnp.concatenate([crecv[e] for e in range(n_e)], axis=0)
    for e in range(TAPS):
        croll[e] = fitted if e == 0 else pltpu.roll(fitted, LANES - e, 1)

    for q in range(groups):
        base = q * tall
        count = min(tall, fc - base)
        if count <= 0:
            continue
        total = jnp.zeros((count, wl), f32)
        for e in range(n_e):
            glow = jnp.zeros((count, wl), f32)
            for t in range(TAPS):
                glow = glow + res2[t, base : base + count, :] * croll[t, e : e + 1, 0:wl]
            left = frecv[e, 0:count, q * wl : (q + 1) * wl] - glow
            outs[e, base : base + count, :] = left
            total = total + left
        mean = total / n_e
        square = jnp.zeros((count, wl), f32)
        for e in range(n_e):
            gone = outs[e, base : base + count, :] - mean
            square = square + gone * gone
        rms_ref[base : base + count, :] = jnp.sqrt(square / n_e + 1e-06)
    out_ref[...] = jnp.swapaxes(outs[...], 0, 1)

    @pl.when(mc > 0)
    def _():
        to_left().wait_send()

    @pl.when(mc < n_c - 1)
    def _():
        to_right().wait_send()

    for copy in sky_out + f_out + g_out + c_out:
        copy.wait_send()


def shards(n_e, n_c, pixels, psf_proj, resolution, basis, sky_fibres, fibre_slot, band_shift):
    fc, band, wl = resolution.shape
    comp, ext = basis.shape
    skyc = sky_fibres.shape[0] // n_c
    own = pixels.shape[1] * pixels.shape[2]
    wave = wl * n_e
    groups = LANES // wl
    per = -(-skyc // groups)
    half = psf_proj.shape[1]
    pitch = -(-half // 8) * 8
    f32, bf16 = jnp.float32, jnp.bfloat16
    anywhere = pl.BlockSpec(memory_space=pl.ANY)
    vmem = pl.BlockSpec(memory_space=pltpu.VMEM)
    smem = pl.BlockSpec(memory_space=pltpu.SMEM)
    dma = pltpu.SemaphoreType.DMA
    scratch = [
        pltpu.VMEM((own + 2 * HALO, LANES), bf16),
        pltpu.VMEM(psf_proj.shape, bf16),
        pltpu.VMEM((band, fc, wl), f32),
        pltpu.VMEM((TAPS, fc, wl), f32),
        pltpu.VMEM((16, wave + LANES), f32),
        pltpu.VMEM((TAPS, 16, wave), f32),
        pltpu.VMEM((per, 16, LANES), f32),
        pltpu.VMEM((per, 16, LANES), bf16),
        pltpu.VMEM((n_e, per, 16, LANES), bf16),
        pltpu.VMEM((skyc, 16, wave), f32),
        pltpu.VMEM((2 * pitch, 2 * LANES), f32),
        pltpu.VMEM((ROWS * SLOTS, 2 * LANES), f32),
        pltpu.VMEM((n_e, SLOTS // groups, LANES), f32),
        pltpu.VMEM((n_e, SLOTS // groups, LANES), f32),
        pltpu.VMEM((n_c, 16, LANES), f32),
        pltpu.VMEM((n_e, 1, LANES), f32),
        pltpu.VMEM((n_e, 1, LANES), f32),
        pltpu.VMEM((TAPS, n_e, LANES), f32),
        pltpu.VMEM((n_e, fc, wl), f32),
        dma((3,)),
        dma((2,)),
        dma((2,)),
    ]
    for size in (n_e, n_e, n_c, n_e):
        scratch += [dma((size,)), dma((size,))]
    cube, rms = pl.pallas_call(
        functools.partial(kernel, n_e, n_c, skyc, comp),
        out_shape=(
            jax.ShapeDtypeStruct((fc, n_e, wl), f32),
            jax.ShapeDtypeStruct((fc, wl), f32),
        ),
        in_specs=[anywhere, anywhere, anywhere, vmem, vmem, vmem, smem, smem, smem],
        out_specs=(vmem, vmem),
        scratch_shapes=scratch,
        compiler_params=pltpu.CompilerParams(
            collective_id=0, has_side_effects=True, vmem_limit_bytes=32 * 1024 * 1024
        ),
        name="extract",
    )(
        pixels.reshape(own, LANES),
        psf_proj,
        jnp.swapaxes(resolution, 0, 1),
        basis,
        fibre_slot.reshape(1, fc),
        band_shift.reshape(1, fc),
        sky_fibres,
        fibre_slot,
        band_shift,
    )
    return jnp.swapaxes(cube, 0, 1), rms


def solution(mesh):
    in_specs = (
        P("exp", "ccd", None, None),
        P("ccd", None, None),
        P("ccd", None, "exp"),
        P(),
        P(),
        P("ccd"),
        P("ccd"),
    )
    out_specs = (P(None, "ccd", "exp"), P("ccd", "exp"))
    body = functools.partial(shards, mesh.shape["exp"], mesh.shape["ccd"])
    return jax.shard_map(body, mesh=mesh, in_specs=in_specs, out_specs=out_specs, check_vma=False)
```

```python
import functools

import jax
import jax.numpy as jnp
from jax import lax
from jax.experimental import pallas as pl
from jax.experimental.pallas import tpu as pltpu
from jax.sharding import PartitionSpec as P

BPIX = 500
MARG = 20
ROWS = 4
BAND = 11
SHIFT = 3
SPAN = 540
LANES = 128
TAPS = BAND + 2 * SHIFT
HALO = MARG * ROWS
DEEP = SPAN * ROWS
SLOTS = 64
SKYROWS = 8
MESH = pl.DeviceIdType.MESH


def column_of(row, count):
    n = row.shape[1]
    sub = lax.broadcasted_iota(jnp.int32, (count, n), 0)
    lane = lax.broadcasted_iota(jnp.int32, (count, n), 1)
    return jnp.sum(jnp.where(sub == lane, row, 0), axis=1, keepdims=True)


def pieces_of(x):
    high = x.astype(jnp.bfloat16)
    rest = x - high.astype(jnp.float32)
    mid = rest.astype(jnp.bfloat16)
    low = (rest - mid.astype(jnp.float32)).astype(jnp.bfloat16)
    return high, mid, low


def kernel(
    n_e, n_c, skyc, comp,
    pix, psf, res, basis_ref, slot_row, shift_row, sky_s, slot_s, shift_s,
    out_ref, rms_ref,
    before, after, res2, bpad, bsh, stage, skysend, skyrecv, skyfull, slots, fluxr,
    fsend, frecv, grecv, csend, crecv, croll, outs,
    halo_ssem, halo_rsem, sky_ssem, sky_rsem, f_ssem, f_rsem,
    g_ssem, g_rsem, c_ssem, c_rsem,
):
    me = lax.axis_index("exp")
    mc = lax.axis_index("ccd")
    fc = res.shape[1]
    wl = res.shape[2]
    own = pix.shape[0]
    inner = before.shape[0] - HALO
    outer = after.shape[0] - HALO
    groups = LANES // wl
    tall = SLOTS // groups
    per = stage.shape[0]
    half = psf.shape[1]
    f32 = jnp.float32

    barrier = pltpu.get_barrier_semaphore()
    for d in range(1, n_e):
        pl.semaphore_signal(
            barrier, inc=1, device_id={"exp": lax.rem(me + d, n_e)}, device_id_type=MESH
        )
    for d in range(1, n_c):
        pl.semaphore_signal(
            barrier, inc=1, device_id={"ccd": lax.rem(mc + d, n_c)}, device_id_type=MESH
        )

    sky = [jnp.clip(sky_s[mc * skyc + i] - mc * fc, 0, fc - 1) for i in range(skyc)]

    stage[...] = jnp.zeros_like(stage)
    bpad[...] = jnp.zeros_like(bpad)
    bpad[0:comp, 0 : basis_ref.shape[1]] = basis_ref[...]
    for i in range(skyc):
        q, s = i // per, i % per
        for d in range(BAND):
            stage[s, d : d + 1, q * wl : (q + 1) * wl] = res[d, pl.ds(sky[i], 1), :]
    skysend[...] = stage[...].astype(jnp.bfloat16)

    pl.semaphore_wait(barrier, n_e - 1 + n_c - 1)

    def to_left():
        return pltpu.make_async_remote_copy(
            src_ref=pix.at[pl.ds(0, HALO)],
            dst_ref=after.at[pl.ds(outer, HALO)],
            send_sem=halo_ssem.at[0],
            recv_sem=halo_rsem.at[0],
            device_id={"ccd": lax.rem(mc + n_c - 1, n_c)},
            device_id_type=MESH,
        )

    def to_right():
        return pltpu.make_async_remote_copy(
            src_ref=pix.at[pl.ds(own - HALO, HALO)],
            dst_ref=before.at[pl.ds(0, HALO)],
            send_sem=halo_ssem.at[1],
            recv_sem=halo_rsem.at[1],
            device_id={"ccd": lax.rem(mc + 1, n_c)},
            device_id_type=MESH,
        )

    @pl.when(mc > 0)
    def _():
        to_left().start()

    @pl.when(mc < n_c - 1)
    def _():
        to_right().start()

    before[HALO:, :] = pix[0:inner, :]
    after[0:outer, :] = pix[own - outer :, :]

    @pl.when(mc == 0)
    def _():
        before[0:HALO, :] = jnp.zeros((HALO, LANES), before.dtype)

    @pl.when(mc == n_c - 1)
    def _():
        after[outer:, :] = jnp.zeros((HALO, LANES), after.dtype)

    def exchange(axis, size, mine, source, landing, ssem, rsem):
        sends, receives = [], []
        for d in range(1, size):
            there = lax.rem(mine + d, size)
            origin = lax.rem(mine + size - d, size)
            sends.append(
                pltpu.make_async_remote_copy(
                    src_ref=source(there), dst_ref=landing.at[mine],
                    send_sem=ssem.at[d], recv_sem=rsem.at[mine],
                    device_id={axis: there}, device_id_type=MESH,
                )
            )
            receives.append(
                pltpu.make_async_remote_copy(
                    src_ref=source(there), dst_ref=landing.at[origin],
                    send_sem=ssem.at[d], recv_sem=rsem.at[origin],
                    device_id={axis: there}, device_id_type=MESH,
                )
            )
        return sends, receives

    sky_out, sky_in = exchange(
        "exp", n_e, me, lambda there: skysend, skyrecv, sky_ssem, sky_rsem
    )
    for copy in sky_out:
        copy.start()
    skyrecv[me] = skysend[...]

    wide = bsh.shape[2]
    for e in range(TAPS):
        bsh[e] = bpad[:, e : e + wide]

    slot = column_of(slot_row[...], SLOTS) - mc * fc
    place = lax.broadcasted_iota(jnp.int32, (SLOTS, 1), 0)
    slot = jnp.where(place < fc, slot, -1000)
    sky_place = lax.broadcasted_iota(jnp.int32, (SKYROWS, 1), 0)
    sky_slot = jnp.full((SKYROWS, 1), -1000, jnp.int32)
    for i in range(skyc):
        sky_slot = jnp.where(sky_place == i, slot_s[sky[i]] - mc * fc, sky_slot)
    gap = slots.shape[0] // 2 - half

    def picker(rows):
        first = rows * ROWS + jnp.where(rows * ROWS >= half, gap, 0)
        lane = lax.broadcasted_iota(jnp.int32, (rows.shape[0], slots.shape[0]), 1)
        return jnp.concatenate(
            [jnp.where(lane == first + r, 1.0, 0.0) for r in range(ROWS)], axis=0
        ).astype(jnp.bfloat16)

    sky_pick, pick = picker(sky_slot), picker(slot)

    slots[...] = jnp.zeros_like(slots)

    def partial(block, lower, upper, window):
        weights = psf[block, :, lower:upper]
        wide_w = weights.astype(f32)
        wide_x = window.astype(f32)
        squares = (wide_w * wide_w).astype(jnp.bfloat16)
        pixvar = (0.25 + wide_x * wide_x).astype(jnp.bfloat16)
        flux = jnp.dot(weights, window, preferred_element_type=f32)
        var = jnp.dot(squares, pixvar, preferred_element_type=f32)
        return flux, var

    blocks = psf.shape[0]
    cuts = []
    for b in range(blocks):
        lower = before.shape[0] if b == 0 else 0
        upper = DEEP - after.shape[0] if b == blocks - 1 else DEEP
        cuts.append((lower, upper))
    main = []
    for b in range(blocks):
        start = b * BPIX * ROWS - HALO
        lower, upper = cuts[b]
        main.append(partial(b, lower, upper, pix[start + lower : start + upper, :]))

    @pl.when(mc < n_c - 1)
    def _():
        to_left().wait_recv()

    @pl.when(mc > 0)
    def _():
        to_right().wait_recv()

    pitch = slots.shape[0] // 2
    for b in range(blocks):
        flux, var = main[b]
        lower, upper = cuts[b]
        if lower > 0:
            more = partial(b, 0, lower, before[...])
            flux, var = flux + more[0], var + more[1]
        if upper < DEEP:
            more = partial(b, upper, DEEP, after[...])
            flux, var = flux + more[0], var + more[1]
        slots[b * pitch : b * pitch + half, 0:LANES] = flux
        slots[b * pitch : b * pitch + half, LANES:] = var

    pieces = pieces_of(slots[...])
    dot = functools.partial(jnp.dot, preferred_element_type=f32)

    def chosen(rows, lower, upper):
        parts = [dot(rows, x[:, lower:upper]) for x in pieces]
        return parts[0] + (parts[1] + parts[2])

    sky_rows = chosen(sky_pick, 0, 2 * LANES)

    for copy in sky_in:
        copy.wait_recv()
    for j in range(n_e):
        block = skyrecv[j].astype(f32)
        for i in range(skyc):
            q, s = i // per, i % per
            skyfull[i, :, j * wl : (j + 1) * wl] = block[s, :, q * wl : (q + 1) * wl]
    sub = lax.broadcasted_iota(jnp.int32, (16, wide), 0)
    sums = [jnp.zeros((16, LANES), f32) for _ in range(comp + 1)]
    for i in range(skyc):
        offset = jnp.clip(shift_s[sky[i]] + SHIFT, 0, 2 * SHIFT)
        model = jnp.zeros((16, wide), f32)
        for d in range(BAND):
            model = model + skyfull[i, d : d + 1, :] * bsh[offset + d]
        rows = [r * SKYROWS + i for r in range(ROWS)]
        flux = jnp.concatenate([sky_rows[x : x + 1, 0:LANES] for x in rows], axis=1)
        var = jnp.concatenate([sky_rows[x : x + 1, LANES:] for x in rows], axis=1)
        full = jnp.where(sub == comp, flux, model)
        weighted = full * (1.0 / var)
        for col in range(comp + 1):
            product = weighted * full[col : col + 1, :]
            for t in range(0, wide, LANES):
                sums[col] = sums[col] + product[:, t : t + LANES]
    lanes16 = lax.broadcasted_iota(jnp.int32, (16, LANES), 1)
    sub16 = lax.broadcasted_iota(jnp.int32, (16, LANES), 0)
    gram = jnp.zeros((16, LANES), f32)
    for col in range(comp + 1):
        gram = jnp.where(lanes16 == col, jnp.sum(sums[col], axis=1, keepdims=True), gram)
    grecv[mc] = gram
    g_out, g_in = exchange(
        "ccd", n_c, mc, lambda there: grecv.at[mc], grecv, g_ssem, g_rsem
    )
    for copy in g_out:
        copy.start()

    fluxr[...] = chosen(pick, 0, LANES)

    for j in range(n_e):
        r, off = j * wl // LANES, j * wl % LANES
        for q in range(groups):
            rows = pl.ds(r * SLOTS + q * tall, tall)
            fsend[j, :, q * wl : (q + 1) * wl] = fluxr[rows, off : off + wl]
    f_out, f_in = exchange(
        "exp", n_e, me, lambda there: fsend.at[there], frecv, f_ssem, f_rsem
    )
    for copy in f_out:
        copy.start()
    frecv[me] = fsend[me]

    planes = [res[d] for d in range(BAND)]
    shift = column_of(shift_row[...], fc) + SHIFT
    for step in (1, 2, 4):
        take = jnp.bitwise_and(shift, step) != 0
        length = min(len(planes) + step, TAPS)
        moved = []
        for e in range(length):
            here = planes[e] if e < len(planes) else jnp.zeros((fc, wl), f32)
            prior = planes[e - step] if e >= step else jnp.zeros((fc, wl), f32)
            moved.append(jnp.where(take, prior, here))
        planes = moved
    for e in range(TAPS):
        res2[e] = planes[e]

    for copy in g_in:
        copy.wait_recv()
    m = grecv[0]
    for c in range(1, n_c):
        m = m + grecv[c]
    for k in range(comp):
        row = m[k : k + 1, :] / m[k : k + 1, k : k + 1]
        m = jnp.where(sub16 == k, row, m - m[:, k : k + 1] * row)
    coeffs = jnp.where(sub16[:, 0:1] < comp, m[:, comp : comp + 1], 0.0)
    spectrum = jnp.sum(coeffs * bpad[...], axis=0, keepdims=True)
    for j in range(n_e):
        csend[j] = spectrum[:, j * wl : j * wl + LANES]
    c_out, c_in = exchange(
        "exp", n_e, me, lambda there: csend.at[there], crecv, c_ssem, c_rsem
    )
    for copy in c_out:
        copy.start()
    crecv[me] = csend[me]
    for copy in f_in:
        copy.wait_recv()
    for copy in c_in:
        copy.wait_recv()

    fitted = jnp.concatenate([crecv[e] for e in range(n_e)], axis=0)
    for e in range(TAPS):
        croll[e] = fitted if e == 0 else pltpu.roll(fitted, LANES - e, 1)

    for q in range(groups):
        base = q * tall
        count = min(tall, fc - base)
        if count <= 0:
            continue
        total = jnp.zeros((count, wl), f32)
        for e in range(n_e):
            glow = jnp.zeros((count, wl), f32)
            for t in range(TAPS):
                glow = glow + res2[t, base : base + count, :] * croll[t, e : e + 1, 0:wl]
            left = frecv[e, 0:count, q * wl : (q + 1) * wl] - glow
            outs[e, base : base + count, :] = left
            total = total + left
        mean = total / n_e
        square = jnp.zeros((count, wl), f32)
        for e in range(n_e):
            gone = outs[e, base : base + count, :] - mean
            square = square + gone * gone
        rms_ref[base : base + count, :] = jnp.sqrt(square / n_e + 1e-06)
    out_ref[...] = jnp.swapaxes(outs[...], 0, 1)

    @pl.when(mc > 0)
    def _():
        to_left().wait_send()

    @pl.when(mc < n_c - 1)
    def _():
        to_right().wait_send()

    for copy in sky_out + f_out + g_out + c_out:
        copy.wait_send()


def deliver(cube_ref, rms_ref, cube_out, rms_out, sem):
    first = pltpu.make_async_copy(cube_ref, cube_out, sem.at[0])
    second = pltpu.make_async_copy(rms_ref, rms_out, sem.at[1])
    first.start()
    second.start()
    first.wait()
    second.wait()


def shards(n_e, n_c, pixels, psf_proj, resolution, basis, sky_fibres, fibre_slot, band_shift):
    fc, band, wl = resolution.shape
    comp, ext = basis.shape
    skyc = sky_fibres.shape[0] // n_c
    own = pixels.shape[1] * pixels.shape[2]
    wave = wl * n_e
    groups = LANES // wl
    per = -(-skyc // groups)
    half = psf_proj.shape[1]
    pitch = -(-half // 8) * 8
    f32, bf16 = jnp.float32, jnp.bfloat16
    anywhere = pl.BlockSpec(memory_space=pl.ANY)
    vmem = pl.BlockSpec(memory_space=pltpu.VMEM)
    smem = pl.BlockSpec(memory_space=pltpu.SMEM)
    dma = pltpu.SemaphoreType.DMA
    scratch = [
        pltpu.VMEM((LANES, LANES), bf16),
        pltpu.VMEM((DEEP - (DEEP - HALO) // LANES * LANES, LANES), bf16),
        pltpu.VMEM((TAPS, fc, wl), f32),
        pltpu.VMEM((16, wave + LANES), f32),
        pltpu.VMEM((TAPS, 16, wave), f32),
        pltpu.VMEM((per, 16, LANES), f32),
        pltpu.VMEM((per, 16, LANES), bf16),
        pltpu.VMEM((n_e, per, 16, LANES), bf16),
        pltpu.VMEM((skyc, 16, wave), f32),
        pltpu.VMEM((2 * pitch, 2 * LANES), f32),
        pltpu.VMEM((ROWS * SLOTS, LANES), f32),
        pltpu.VMEM((n_e, SLOTS // groups, LANES), f32),
        pltpu.VMEM((n_e, SLOTS // groups, LANES), f32),
        pltpu.VMEM((n_c, 16, LANES), f32),
        pltpu.VMEM((n_e, 1, LANES), f32),
        pltpu.VMEM((n_e, 1, LANES), f32),
        pltpu.VMEM((TAPS, n_e, LANES), f32),
        pltpu.VMEM((n_e, fc, wl), f32),
        dma((2,)),
        dma((2,)),
    ]
    for size in (n_e, n_e, n_c, n_e):
        scratch += [dma((size,)), dma((size,))]
    cube, rms = pl.pallas_call(
        functools.partial(kernel, n_e, n_c, skyc, comp),
        out_shape=(
            jax.ShapeDtypeStruct((fc, n_e, wl), f32),
            jax.ShapeDtypeStruct((fc, wl), f32),
        ),
        in_specs=[vmem, vmem, vmem, vmem, vmem, vmem, smem, smem, smem],
        out_specs=(vmem, vmem),
        scratch_shapes=scratch,
        compiler_params=pltpu.CompilerParams(
            collective_id=0, has_side_effects=True, vmem_limit_bytes=32 * 1024 * 1024
        ),
        name="extract",
    )(
        pixels.reshape(own, LANES),
        psf_proj,
        jnp.swapaxes(resolution, 0, 1),
        basis,
        fibre_slot.reshape(1, fc),
        band_shift.reshape(1, fc),
        sky_fibres,
        fibre_slot,
        band_shift,
    )
    cube, rms = pl.pallas_call(
        deliver,
        out_shape=(
            jax.ShapeDtypeStruct(cube.shape, f32),
            jax.ShapeDtypeStruct(rms.shape, f32),
        ),
        in_specs=[anywhere, anywhere],
        out_specs=(anywhere, anywhere),
        scratch_shapes=[dma((2,))],
        name="deliver",
    )(cube, rms)
    return jnp.swapaxes(cube, 0, 1), rms


def solution(mesh):
    in_specs = (
        P("exp", "ccd", None, None),
        P("ccd", None, None),
        P("ccd", None, "exp"),
        P(),
        P(),
        P("ccd"),
        P("ccd"),
    )
    out_specs = (P(None, "ccd", "exp"), P("ccd", "exp"))
    body = functools.partial(shards, mesh.shape["exp"], mesh.shape["ccd"])
    return jax.shard_map(body, mesh=mesh, in_specs=in_specs, out_specs=out_specs, check_vma=False)
```

```python
import functools

import jax
import jax.numpy as jnp
from jax import lax
from jax.experimental import pallas as pl
from jax.experimental.pallas import tpu as pltpu
from jax.sharding import PartitionSpec as P

BPIX = 500
MARG = 20
ROWS = 4
BAND = 11
SHIFT = 3
SPAN = 540
LANES = 128
TAPS = BAND + 2 * SHIFT
HALO = MARG * ROWS
DEEP = SPAN * ROWS
SLOTS = 64
SKYROWS = 8
MESH = pl.DeviceIdType.MESH


def column_of(row, count):
    n = row.shape[1]
    sub = lax.broadcasted_iota(jnp.int32, (count, n), 0)
    lane = lax.broadcasted_iota(jnp.int32, (count, n), 1)
    return jnp.sum(jnp.where(sub == lane, row, 0), axis=1, keepdims=True)


def pieces_of(x):
    high = x.astype(jnp.bfloat16)
    rest = x - high.astype(jnp.float32)
    mid = rest.astype(jnp.bfloat16)
    low = (rest - mid.astype(jnp.float32)).astype(jnp.bfloat16)
    return high, mid, low


def kernel(
    n_e, n_c, skyc, comp,
    pix, psf, res, basis_ref, slot_row, shift_row, sky_s, slot_s, shift_s,
    out_ref, rms_ref,
    before, after, res2, bpad, bsh, stage, skysend, skyrecv, skyfull, slots, fluxr,
    fsend, frecv, grecv, csend, crecv, croll, outs,
    halo_ssem, halo_rsem, sky_ssem, sky_rsem, f_ssem, f_rsem,
    g_ssem, g_rsem, c_ssem, c_rsem,
):
    me = lax.axis_index("exp")
    mc = lax.axis_index("ccd")
    fc = res.shape[1]
    wl = res.shape[2]
    own = pix.shape[0]
    inner = before.shape[0] - HALO
    outer = after.shape[0] - HALO
    groups = LANES // wl
    tall = SLOTS // groups
    per = stage.shape[0]
    half = psf.shape[1]
    f32 = jnp.float32

    barrier = pltpu.get_barrier_semaphore()
    for d in range(1, n_e):
        pl.semaphore_signal(
            barrier, inc=1, device_id={"exp": lax.rem(me + d, n_e)}, device_id_type=MESH
        )
    for d in range(1, n_c):
        pl.semaphore_signal(
            barrier, inc=1, device_id={"ccd": lax.rem(mc + d, n_c)}, device_id_type=MESH
        )

    sky = [jnp.clip(sky_s[mc * skyc + i] - mc * fc, 0, fc - 1) for i in range(skyc)]

    stage[...] = jnp.zeros_like(stage)
    bpad[...] = jnp.zeros_like(bpad)
    bpad[0:comp, 0 : basis_ref.shape[1]] = basis_ref[...]
    for i in range(skyc):
        q, s = i // per, i % per
        for d in range(BAND):
            stage[s, d : d + 1, q * wl : (q + 1) * wl] = res[d, pl.ds(sky[i], 1), :]
    skysend[...] = stage[...].astype(jnp.bfloat16)

    pl.semaphore_wait(barrier, n_e - 1 + n_c - 1)

    def to_left():
        return pltpu.make_async_remote_copy(
            src_ref=pix.at[pl.ds(0, HALO)],
            dst_ref=after.at[pl.ds(outer, HALO)],
            send_sem=halo_ssem.at[0],
            recv_sem=halo_rsem.at[0],
            device_id={"ccd": lax.rem(mc + n_c - 1, n_c)},
            device_id_type=MESH,
        )

    def to_right():
        return pltpu.make_async_remote_copy(
            src_ref=pix.at[pl.ds(own - HALO, HALO)],
            dst_ref=before.at[pl.ds(0, HALO)],
            send_sem=halo_ssem.at[1],
            recv_sem=halo_rsem.at[1],
            device_id={"ccd": lax.rem(mc + 1, n_c)},
            device_id_type=MESH,
        )

    @pl.when(mc > 0)
    def _():
        to_left().start()

    @pl.when(mc < n_c - 1)
    def _():
        to_right().start()

    before[HALO:, :] = pix[0:inner, :]
    after[0:outer, :] = pix[own - outer :, :]

    @pl.when(mc == 0)
    def _():
        before[0:HALO, :] = jnp.zeros((HALO, LANES), before.dtype)

    @pl.when(mc == n_c - 1)
    def _():
        after[outer:, :] = jnp.zeros((HALO, LANES), after.dtype)

    def exchange(axis, size, mine, source, landing, ssem, rsem):
        sends, receives = [], []
        for d in range(1, size):
            there = lax.rem(mine + d, size)
            origin = lax.rem(mine + size - d, size)
            sends.append(
                pltpu.make_async_remote_copy(
                    src_ref=source(there), dst_ref=landing.at[mine],
                    send_sem=ssem.at[d], recv_sem=rsem.at[mine],
                    device_id={axis: there}, device_id_type=MESH,
                )
            )
            receives.append(
                pltpu.make_async_remote_copy(
                    src_ref=source(there), dst_ref=landing.at[origin],
                    send_sem=ssem.at[d], recv_sem=rsem.at[origin],
                    device_id={axis: there}, device_id_type=MESH,
                )
            )
        return sends, receives

    sky_out, sky_in = exchange(
        "exp", n_e, me, lambda there: skysend, skyrecv, sky_ssem, sky_rsem
    )
    for copy in sky_out:
        copy.start()
    skyrecv[me] = skysend[...]

    wide = bsh.shape[2]
    for e in range(TAPS):
        bsh[e] = bpad[:, e : e + wide]

    slot = column_of(slot_row[...], SLOTS) - mc * fc
    place = lax.broadcasted_iota(jnp.int32, (SLOTS, 1), 0)
    slot = jnp.where(place < fc, slot, -1000)
    sky_place = lax.broadcasted_iota(jnp.int32, (SKYROWS, 1), 0)
    sky_slot = jnp.full((SKYROWS, 1), -1000, jnp.int32)
    for i in range(skyc):
        sky_slot = jnp.where(sky_place == i, slot_s[sky[i]] - mc * fc, sky_slot)
    gap = slots.shape[0] // 2 - half

    def picker(rows):
        first = rows * ROWS + jnp.where(rows * ROWS >= half, gap, 0)
        lane = lax.broadcasted_iota(jnp.int32, (rows.shape[0], slots.shape[0]), 1)
        return jnp.concatenate(
            [jnp.where(lane == first + r, 1.0, 0.0) for r in range(ROWS)], axis=0
        ).astype(jnp.bfloat16)

    sky_pick, pick = picker(sky_slot), picker(slot)

    slots[...] = jnp.zeros_like(slots)

    def partial(block, lower, upper, window):
        weights = psf[block, :, lower:upper]
        wide_w = weights.astype(f32)
        wide_x = window.astype(f32)
        squares = (wide_w * wide_w).astype(jnp.bfloat16)
        pixvar = (0.25 + wide_x * wide_x).astype(jnp.bfloat16)
        flux = jnp.dot(weights, window, preferred_element_type=f32)
        var = jnp.dot(squares, pixvar, preferred_element_type=f32)
        return flux, var

    blocks = psf.shape[0]
    cuts = []
    for b in range(blocks):
        lower = before.shape[0] if b == 0 else 0
        upper = DEEP - after.shape[0] if b == blocks - 1 else DEEP
        cuts.append((lower, upper))
    main = []
    for b in range(blocks):
        start = b * BPIX * ROWS - HALO
        lower, upper = cuts[b]
        main.append(partial(b, lower, upper, pix[start + lower : start + upper, :]))

    @pl.when(mc < n_c - 1)
    def _():
        to_left().wait_recv()

    @pl.when(mc > 0)
    def _():
        to_right().wait_recv()

    pitch = slots.shape[0] // 2
    for b in range(blocks):
        flux, var = main[b]
        lower, upper = cuts[b]
        if lower > 0:
            more = partial(b, 0, lower, before[...])
            flux, var = flux + more[0], var + more[1]
        if upper < DEEP:
            more = partial(b, upper, DEEP, after[...])
            flux, var = flux + more[0], var + more[1]
        slots[b * pitch : b * pitch + half, 0:LANES] = flux
        slots[b * pitch : b * pitch + half, LANES:] = var

    pieces = pieces_of(slots[...])
    dot = functools.partial(jnp.dot, preferred_element_type=f32)

    def chosen(rows, lower, upper):
        parts = [dot(rows, x[:, lower:upper]) for x in pieces]
        return parts[0] + (parts[1] + parts[2])

    sky_rows = chosen(sky_pick, 0, 2 * LANES)

    fluxr[...] = chosen(pick, 0, LANES)

    for j in range(n_e):
        r, off = j * wl // LANES, j * wl % LANES
        for q in range(groups):
            rows = pl.ds(r * SLOTS + q * tall, tall)
            fsend[j, :, q * wl : (q + 1) * wl] = fluxr[rows, off : off + wl]
    f_out, f_in = exchange(
        "exp", n_e, me, lambda there: fsend.at[there], frecv, f_ssem, f_rsem
    )
    for copy in f_out:
        copy.start()
    frecv[me] = fsend[me]

    for copy in sky_in:
        copy.wait_recv()
    for j in range(n_e):
        block = skyrecv[j].astype(f32)
        for i in range(skyc):
            q, s = i // per, i % per
            skyfull[i, :, j * wl : (j + 1) * wl] = block[s, :, q * wl : (q + 1) * wl]
    sub = lax.broadcasted_iota(jnp.int32, (16, wide), 0)
    sums = [jnp.zeros((16, LANES), f32) for _ in range(comp + 1)]
    for i in range(skyc):
        offset = jnp.clip(shift_s[sky[i]] + SHIFT, 0, 2 * SHIFT)
        model = jnp.zeros((16, wide), f32)
        for d in range(BAND):
            model = model + skyfull[i, d : d + 1, :] * bsh[offset + d]
        rows = [r * SKYROWS + i for r in range(ROWS)]
        flux = jnp.concatenate([sky_rows[x : x + 1, 0:LANES] for x in rows], axis=1)
        var = jnp.concatenate([sky_rows[x : x + 1, LANES:] for x in rows], axis=1)
        full = jnp.where(sub == comp, flux, model)
        weighted = full * (1.0 / var)
        for col in range(comp + 1):
            product = weighted * full[col : col + 1, :]
            for t in range(0, wide, LANES):
                sums[col] = sums[col] + product[:, t : t + LANES]
    lanes16 = lax.broadcasted_iota(jnp.int32, (16, LANES), 1)
    sub16 = lax.broadcasted_iota(jnp.int32, (16, LANES), 0)
    gram = jnp.zeros((16, LANES), f32)
    for col in range(comp + 1):
        gram = jnp.where(lanes16 == col, jnp.sum(sums[col], axis=1, keepdims=True), gram)
    grecv[mc] = gram
    g_out, g_in = exchange(
        "ccd", n_c, mc, lambda there: grecv.at[mc], grecv, g_ssem, g_rsem
    )
    for copy in g_out:
        copy.start()

    planes = [res[d] for d in range(BAND)]
    shift = column_of(shift_row[...], fc) + SHIFT
    for step in (1, 2, 4):
        take = jnp.bitwise_and(shift, step) != 0
        length = min(len(planes) + step, TAPS)
        moved = []
        for e in range(length):
            here = planes[e] if e < len(planes) else jnp.zeros((fc, wl), f32)
            prior = planes[e - step] if e >= step else jnp.zeros((fc, wl), f32)
            moved.append(jnp.where(take, prior, here))
        planes = moved
    for e in range(TAPS):
        res2[e] = planes[e]

    for copy in g_in:
        copy.wait_recv()
    m = grecv[0]
    for c in range(1, n_c):
        m = m + grecv[c]
    for k in range(comp):
        row = m[k : k + 1, :] / m[k : k + 1, k : k + 1]
        m = jnp.where(sub16 == k, row, m - m[:, k : k + 1] * row)
    coeffs = jnp.where(sub16[:, 0:1] < comp, m[:, comp : comp + 1], 0.0)
    spectrum = jnp.sum(coeffs * bpad[...], axis=0, keepdims=True)
    for j in range(n_e):
        csend[j] = spectrum[:, j * wl : j * wl + LANES]
    c_out, c_in = exchange(
        "exp", n_e, me, lambda there: csend.at[there], crecv, c_ssem, c_rsem
    )
    for copy in c_out:
        copy.start()
    crecv[me] = csend[me]
    for copy in f_in:
        copy.wait_recv()
    for copy in c_in:
        copy.wait_recv()

    fitted = jnp.concatenate([crecv[e] for e in range(n_e)], axis=0)
    for e in range(TAPS):
        croll[e] = fitted if e == 0 else pltpu.roll(fitted, LANES - e, 1)

    for q in range(groups):
        base = q * tall
        count = min(tall, fc - base)
        if count <= 0:
            continue
        total = jnp.zeros((count, wl), f32)
        for e in range(n_e):
            glow = jnp.zeros((count, wl), f32)
            for t in range(TAPS):
                glow = glow + res2[t, base : base + count, :] * croll[t, e : e + 1, 0:wl]
            left = frecv[e, 0:count, q * wl : (q + 1) * wl] - glow
            outs[e, base : base + count, :] = left
            total = total + left
        mean = total / n_e
        square = jnp.zeros((count, wl), f32)
        for e in range(n_e):
            gone = outs[e, base : base + count, :] - mean
            square = square + gone * gone
        rms_ref[base : base + count, :] = jnp.sqrt(square / n_e + 1e-06)
    out_ref[...] = jnp.swapaxes(outs[...], 0, 1)

    @pl.when(mc > 0)
    def _():
        to_left().wait_send()

    @pl.when(mc < n_c - 1)
    def _():
        to_right().wait_send()

    for copy in sky_out + f_out + g_out + c_out:
        copy.wait_send()


def deliver(cube_ref, rms_ref, cube_out, rms_out, sem):
    first = pltpu.make_async_copy(cube_ref, cube_out, sem.at[0])
    second = pltpu.make_async_copy(rms_ref, rms_out, sem.at[1])
    first.start()
    second.start()
    first.wait()
    second.wait()


def shards(n_e, n_c, pixels, psf_proj, resolution, basis, sky_fibres, fibre_slot, band_shift):
    fc, band, wl = resolution.shape
    comp, ext = basis.shape
    skyc = sky_fibres.shape[0] // n_c
    own = pixels.shape[1] * pixels.shape[2]
    wave = wl * n_e
    groups = LANES // wl
    per = -(-skyc // groups)
    half = psf_proj.shape[1]
    pitch = -(-half // 8) * 8
    f32, bf16 = jnp.float32, jnp.bfloat16
    anywhere = pl.BlockSpec(memory_space=pl.ANY)
    vmem = pl.BlockSpec(memory_space=pltpu.VMEM)
    smem = pl.BlockSpec(memory_space=pltpu.SMEM)
    dma = pltpu.SemaphoreType.DMA
    scratch = [
        pltpu.VMEM((LANES, LANES), bf16),
        pltpu.VMEM((DEEP - (DEEP - HALO) // LANES * LANES, LANES), bf16),
        pltpu.VMEM((TAPS, fc, wl), f32),
        pltpu.VMEM((16, wave + LANES), f32),
        pltpu.VMEM((TAPS, 16, wave), f32),
        pltpu.VMEM((per, 16, LANES), f32),
        pltpu.VMEM((per, 16, LANES), bf16),
        pltpu.VMEM((n_e, per, 16, LANES), bf16),
        pltpu.VMEM((skyc, 16, wave), f32),
        pltpu.VMEM((2 * pitch, 2 * LANES), f32),
        pltpu.VMEM((ROWS * SLOTS, LANES), f32),
        pltpu.VMEM((n_e, SLOTS // groups, LANES), f32),
        pltpu.VMEM((n_e, SLOTS // groups, LANES), f32),
        pltpu.VMEM((n_c, 16, LANES), f32),
        pltpu.VMEM((n_e, 1, LANES), f32),
        pltpu.VMEM((n_e, 1, LANES), f32),
        pltpu.VMEM((TAPS, n_e, LANES), f32),
        pltpu.VMEM((n_e, fc, wl), f32),
        dma((2,)),
        dma((2,)),
    ]
    for size in (n_e, n_e, n_c, n_e):
        scratch += [dma((size,)), dma((size,))]
    cube, rms = pl.pallas_call(
        functools.partial(kernel, n_e, n_c, skyc, comp),
        out_shape=(
            jax.ShapeDtypeStruct((fc, n_e, wl), f32),
            jax.ShapeDtypeStruct((fc, wl), f32),
        ),
        in_specs=[vmem, vmem, vmem, vmem, vmem, vmem, smem, smem, smem],
        out_specs=(vmem, vmem),
        scratch_shapes=scratch,
        compiler_params=pltpu.CompilerParams(
            collective_id=0, has_side_effects=True, vmem_limit_bytes=32 * 1024 * 1024
        ),
        name="extract",
    )(
        pixels.reshape(own, LANES),
        psf_proj,
        jnp.swapaxes(resolution, 0, 1),
        basis,
        fibre_slot.reshape(1, fc),
        band_shift.reshape(1, fc),
        sky_fibres,
        fibre_slot,
        band_shift,
    )
    cube, rms = pl.pallas_call(
        deliver,
        out_shape=(
            jax.ShapeDtypeStruct(cube.shape, f32),
            jax.ShapeDtypeStruct(rms.shape, f32),
        ),
        in_specs=[vmem, vmem],
        out_specs=(anywhere, anywhere),
        scratch_shapes=[dma((2,))],
        name="deliver",
    )(cube, rms)
    return jnp.swapaxes(cube, 0, 1), rms


def solution(mesh):
    in_specs = (
        P("exp", "ccd", None, None),
        P("ccd", None, None),
        P("ccd", None, "exp"),
        P(),
        P(),
        P("ccd"),
        P("ccd"),
    )
    out_specs = (P(None, "ccd", "exp"), P("ccd", "exp"))
    body = functools.partial(shards, mesh.shape["exp"], mesh.shape["ccd"])
    return jax.shard_map(body, mesh=mesh, in_specs=in_specs, out_specs=out_specs, check_vma=False)
```

```python
import functools

import jax
import jax.numpy as jnp
from jax import lax
from jax.experimental import pallas as pl
from jax.experimental.pallas import tpu as pltpu
from jax.sharding import PartitionSpec as P

BPIX = 500
MARG = 20
ROWS = 4
BAND = 11
SHIFT = 3
SPAN = 540
LANES = 128
TAPS = BAND + 2 * SHIFT
HALO = MARG * ROWS
DEEP = SPAN * ROWS
SLOTS = 64
SKYROWS = 8
MESH = pl.DeviceIdType.MESH


def column_of(row, count):
    n = row.shape[1]
    sub = lax.broadcasted_iota(jnp.int32, (count, n), 0)
    lane = lax.broadcasted_iota(jnp.int32, (count, n), 1)
    return jnp.sum(jnp.where(sub == lane, row, 0), axis=1, keepdims=True)


def pieces_of(x):
    high = x.astype(jnp.bfloat16)
    rest = x - high.astype(jnp.float32)
    mid = rest.astype(jnp.bfloat16)
    low = (rest - mid.astype(jnp.float32)).astype(jnp.bfloat16)
    return high, mid, low


def kernel(
    n_e, n_c, skyc, comp,
    pix, psf, res, basis_ref, slot_row, shift_row, sky_s, slot_s, shift_s,
    out_ref, rms_ref,
    before, after, res2, bpad, bsh, stage, skysend, skyrecv, skyfull, slots, fluxr,
    fsend, frecv, grecv, csend, crecv, croll, outs,
    halo_ssem, halo_rsem, sky_ssem, sky_rsem, f_ssem, f_rsem,
    g_ssem, g_rsem, c_ssem, c_rsem,
):
    me = lax.axis_index("exp")
    mc = lax.axis_index("ccd")
    fc = res.shape[1]
    wl = res.shape[2]
    own = pix.shape[0]
    inner = before.shape[0] - HALO
    outer = after.shape[0] - HALO
    groups = LANES // wl
    tall = SLOTS // groups
    per = stage.shape[0]
    half = psf.shape[1]
    f32 = jnp.float32

    barrier = pltpu.get_barrier_semaphore()
    for d in range(1, n_e):
        pl.semaphore_signal(
            barrier, inc=1, device_id={"exp": lax.rem(me + d, n_e)}, device_id_type=MESH
        )
    for d in range(1, n_c):
        pl.semaphore_signal(
            barrier, inc=1, device_id={"ccd": lax.rem(mc + d, n_c)}, device_id_type=MESH
        )

    sky = [jnp.clip(sky_s[mc * skyc + i] - mc * fc, 0, fc - 1) for i in range(skyc)]

    stage[...] = jnp.zeros_like(stage)
    bpad[...] = jnp.zeros_like(bpad)
    bpad[0:comp, 0 : basis_ref.shape[1]] = basis_ref[...]
    for i in range(skyc):
        q, s = i // per, i % per
        for d in range(BAND):
            stage[s, d : d + 1, q * wl : (q + 1) * wl] = res[d, pl.ds(sky[i], 1), :]
    skysend[...] = stage[...].astype(jnp.bfloat16)

    pl.semaphore_wait(barrier, n_e - 1 + n_c - 1)

    def to_left():
        return pltpu.make_async_remote_copy(
            src_ref=pix.at[pl.ds(0, HALO)],
            dst_ref=after.at[pl.ds(outer, HALO)],
            send_sem=halo_ssem.at[0],
            recv_sem=halo_rsem.at[0],
            device_id={"ccd": lax.rem(mc + n_c - 1, n_c)},
            device_id_type=MESH,
        )

    def to_right():
        return pltpu.make_async_remote_copy(
            src_ref=pix.at[pl.ds(own - HALO, HALO)],
            dst_ref=before.at[pl.ds(0, HALO)],
            send_sem=halo_ssem.at[1],
            recv_sem=halo_rsem.at[1],
            device_id={"ccd": lax.rem(mc + 1, n_c)},
            device_id_type=MESH,
        )

    @pl.when(mc > 0)
    def _():
        to_left().start()

    @pl.when(mc < n_c - 1)
    def _():
        to_right().start()

    before[HALO:, :] = pix[0:inner, :]
    after[0:outer, :] = pix[own - outer :, :]

    @pl.when(mc == 0)
    def _():
        before[0:HALO, :] = jnp.zeros((HALO, LANES), before.dtype)

    @pl.when(mc == n_c - 1)
    def _():
        after[outer:, :] = jnp.zeros((HALO, LANES), after.dtype)

    def exchange(axis, size, mine, source, landing, ssem, rsem):
        sends, receives = [], []
        for d in range(1, size):
            there = lax.rem(mine + d, size)
            origin = lax.rem(mine + size - d, size)
            sends.append(
                pltpu.make_async_remote_copy(
                    src_ref=source(there), dst_ref=landing.at[mine],
                    send_sem=ssem.at[d], recv_sem=rsem.at[mine],
                    device_id={axis: there}, device_id_type=MESH,
                )
            )
            receives.append(
                pltpu.make_async_remote_copy(
                    src_ref=source(there), dst_ref=landing.at[origin],
                    send_sem=ssem.at[d], recv_sem=rsem.at[origin],
                    device_id={axis: there}, device_id_type=MESH,
                )
            )
        return sends, receives

    sky_out, sky_in = exchange(
        "exp", n_e, me, lambda there: skysend, skyrecv, sky_ssem, sky_rsem
    )
    for copy in sky_out:
        copy.start()
    skyrecv[me] = skysend[...]

    wide = bsh.shape[2]
    for e in range(TAPS):
        bsh[e] = bpad[:, e : e + wide]

    slot = column_of(slot_row[...], SLOTS) - mc * fc
    place = lax.broadcasted_iota(jnp.int32, (SLOTS, 1), 0)
    slot = jnp.where(place < fc, slot, -1000)
    sky_place = lax.broadcasted_iota(jnp.int32, (SKYROWS, 1), 0)
    sky_slot = jnp.full((SKYROWS, 1), -1000, jnp.int32)
    for i in range(skyc):
        sky_slot = jnp.where(sky_place == i, slot_s[sky[i]] - mc * fc, sky_slot)
    gap = slots.shape[0] // 2 - half

    def picker(rows):
        first = rows * ROWS + jnp.where(rows * ROWS >= half, gap, 0)
        lane = lax.broadcasted_iota(jnp.int32, (rows.shape[0], slots.shape[0]), 1)
        return jnp.concatenate(
            [jnp.where(lane == first + r, 1.0, 0.0) for r in range(ROWS)], axis=0
        ).astype(jnp.bfloat16)

    sky_pick, pick = picker(sky_slot), picker(slot)

    slots[...] = jnp.zeros_like(slots)

    def partial(block, lower, upper, window):
        weights = psf[block, :, lower:upper]
        wide_w = weights.astype(f32)
        wide_x = window.astype(f32)
        squares = (wide_w * wide_w).astype(jnp.bfloat16)
        pixvar = (0.25 + wide_x * wide_x).astype(jnp.bfloat16)
        flux = jnp.dot(weights, window, preferred_element_type=f32)
        var = jnp.dot(squares, pixvar, preferred_element_type=f32)
        return flux, var

    blocks = psf.shape[0]
    cuts = []
    for b in range(blocks):
        lower = before.shape[0] if b == 0 else 0
        upper = DEEP - after.shape[0] if b == blocks - 1 else DEEP
        cuts.append((lower, upper))
    main = []
    for b in range(blocks):
        start = b * BPIX * ROWS - HALO
        lower, upper = cuts[b]
        main.append(partial(b, lower, upper, pix[start + lower : start + upper, :]))

    @pl.when(mc < n_c - 1)
    def _():
        to_left().wait_recv()

    @pl.when(mc > 0)
    def _():
        to_right().wait_recv()

    pitch = slots.shape[0] // 2
    for b in range(blocks):
        flux, var = main[b]
        lower, upper = cuts[b]
        if lower > 0:
            more = partial(b, 0, lower, before[...])
            flux, var = flux + more[0], var + more[1]
        if upper < DEEP:
            more = partial(b, upper, DEEP, after[...])
            flux, var = flux + more[0], var + more[1]
        slots[b * pitch : b * pitch + half, 0:LANES] = flux
        slots[b * pitch : b * pitch + half, LANES:] = var

    pieces = pieces_of(slots[...])
    dot = functools.partial(jnp.dot, preferred_element_type=f32)

    def chosen(rows, lower, upper):
        parts = [dot(rows, x[:, lower:upper]) for x in pieces]
        return parts[0] + (parts[1] + parts[2])

    sky_rows = chosen(sky_pick, 0, 2 * LANES)

    fluxr[...] = chosen(pick, 0, LANES)

    for j in range(n_e):
        r, off = j * wl // LANES, j * wl % LANES
        for q in range(groups):
            rows = pl.ds(r * SLOTS + q * tall, tall)
            fsend[j, :, q * wl : (q + 1) * wl] = fluxr[rows, off : off + wl]
    f_out, f_in = exchange(
        "exp", n_e, me, lambda there: fsend.at[there], frecv, f_ssem, f_rsem
    )
    for copy in f_out:
        copy.start()
    frecv[me] = fsend[me]

    for copy in sky_in:
        copy.wait_recv()
    for j in range(n_e):
        block = skyrecv[j].astype(f32)
        for i in range(skyc):
            q, s = i // per, i % per
            skyfull[i, :, j * wl : (j + 1) * wl] = block[s, :, q * wl : (q + 1) * wl]
    sub = lax.broadcasted_iota(jnp.int32, (16, wide), 0)
    sums = [jnp.zeros((16, LANES), f32) for _ in range(comp + 1)]
    for i in range(skyc):
        offset = jnp.clip(shift_s[sky[i]] + SHIFT, 0, 2 * SHIFT)
        model = jnp.zeros((16, wide), f32)
        for d in range(BAND):
            model = model + skyfull[i, d : d + 1, :] * bsh[offset + d]
        rows = [r * SKYROWS + i for r in range(ROWS)]
        flux = jnp.concatenate([sky_rows[x : x + 1, 0:LANES] for x in rows], axis=1)
        var = jnp.concatenate([sky_rows[x : x + 1, LANES:] for x in rows], axis=1)
        full = jnp.where(sub == comp, flux, model)
        weighted = full * (1.0 / var)
        for col in range(comp + 1):
            product = weighted * full[col : col + 1, :]
            for t in range(0, wide, LANES):
                sums[col] = sums[col] + product[:, t : t + LANES]
    lanes16 = lax.broadcasted_iota(jnp.int32, (16, LANES), 1)
    sub16 = lax.broadcasted_iota(jnp.int32, (16, LANES), 0)
    gram = jnp.zeros((16, LANES), f32)
    for col in range(comp + 1):
        gram = jnp.where(lanes16 == col, jnp.sum(sums[col], axis=1, keepdims=True), gram)
    grecv[mc] = gram
    g_out, g_in = exchange(
        "ccd", n_c, mc, lambda there: grecv.at[mc], grecv, g_ssem, g_rsem
    )
    for copy in g_out:
        copy.start()

    planes = [res[d] for d in range(BAND)]
    shift = column_of(shift_row[...], fc) + SHIFT
    for step in (1, 2, 4):
        take = jnp.bitwise_and(shift, step) != 0
        length = min(len(planes) + step, TAPS)
        moved = []
        for e in range(length):
            here = planes[e] if e < len(planes) else jnp.zeros((fc, wl), f32)
            prior = planes[e - step] if e >= step else jnp.zeros((fc, wl), f32)
            moved.append(jnp.where(take, prior, here))
        planes = moved
    for e in range(TAPS):
        res2[e] = planes[e]

    for copy in g_in:
        copy.wait_recv()
    m = grecv[0]
    for c in range(1, n_c):
        m = m + grecv[c]
    for k in range(comp):
        row = m[k : k + 1, :] / m[k : k + 1, k : k + 1]
        m = jnp.where(sub16 == k, row, m - m[:, k : k + 1] * row)
    coeffs = jnp.where(sub16[:, 0:1] < comp, m[:, comp : comp + 1], 0.0)
    spectrum = jnp.sum(coeffs * bpad[...], axis=0, keepdims=True)
    for j in range(n_e):
        csend[j] = spectrum[:, j * wl : j * wl + LANES]
    c_out, c_in = exchange(
        "exp", n_e, me, lambda there: csend.at[there], crecv, c_ssem, c_rsem
    )
    for copy in c_out:
        copy.start()
    crecv[me] = csend[me]
    for copy in f_in:
        copy.wait_recv()
    for copy in c_in:
        copy.wait_recv()

    fitted = jnp.concatenate([crecv[e] for e in range(n_e)], axis=0)
    for e in range(TAPS):
        croll[e] = fitted if e == 0 else pltpu.roll(fitted, LANES - e, 1)

    for q in range(groups):
        base = q * tall
        count = min(tall, fc - base)
        if count <= 0:
            continue
        total = jnp.zeros((count, wl), f32)
        for e in range(n_e):
            glow = jnp.zeros((count, wl), f32)
            for t in range(TAPS):
                glow = glow + res2[t, base : base + count, :] * croll[t, e : e + 1, 0:wl]
            left = frecv[e, 0:count, q * wl : (q + 1) * wl] - glow
            outs[e, base : base + count, :] = left
            total = total + left
        mean = total / n_e
        square = jnp.zeros((count, wl), f32)
        for e in range(n_e):
            gone = outs[e, base : base + count, :] - mean
            square = square + gone * gone
        rms_ref[base : base + count, :] = jnp.sqrt(square / n_e + 1e-06)
    out_ref[...] = jnp.swapaxes(outs[...], 0, 1)

    @pl.when(mc > 0)
    def _():
        to_left().wait_send()

    @pl.when(mc < n_c - 1)
    def _():
        to_right().wait_send()

    for copy in sky_out + f_out + g_out + c_out:
        copy.wait_send()


def shards(n_e, n_c, pixels, psf_proj, resolution, basis, sky_fibres, fibre_slot, band_shift):
    fc, band, wl = resolution.shape
    comp, ext = basis.shape
    skyc = sky_fibres.shape[0] // n_c
    own = pixels.shape[1] * pixels.shape[2]
    wave = wl * n_e
    groups = LANES // wl
    per = -(-skyc // groups)
    half = psf_proj.shape[1]
    pitch = -(-half // 8) * 8
    f32, bf16 = jnp.float32, jnp.bfloat16
    vmem = pl.BlockSpec(memory_space=pltpu.VMEM)
    smem = pl.BlockSpec(memory_space=pltpu.SMEM)
    dma = pltpu.SemaphoreType.DMA
    scratch = [
        pltpu.VMEM((LANES, LANES), bf16),
        pltpu.VMEM((DEEP - (DEEP - HALO) // LANES * LANES, LANES), bf16),
        pltpu.VMEM((TAPS, fc, wl), f32),
        pltpu.VMEM((16, wave + LANES), f32),
        pltpu.VMEM((TAPS, 16, wave), f32),
        pltpu.VMEM((per, 16, LANES), f32),
        pltpu.VMEM((per, 16, LANES), bf16),
        pltpu.VMEM((n_e, per, 16, LANES), bf16),
        pltpu.VMEM((skyc, 16, wave), f32),
        pltpu.VMEM((2 * pitch, 2 * LANES), f32),
        pltpu.VMEM((ROWS * SLOTS, LANES), f32),
        pltpu.VMEM((n_e, SLOTS // groups, LANES), f32),
        pltpu.VMEM((n_e, SLOTS // groups, LANES), f32),
        pltpu.VMEM((n_c, 16, LANES), f32),
        pltpu.VMEM((n_e, 1, LANES), f32),
        pltpu.VMEM((n_e, 1, LANES), f32),
        pltpu.VMEM((TAPS, n_e, LANES), f32),
        pltpu.VMEM((n_e, fc, wl), f32),
        dma((2,)),
        dma((2,)),
    ]
    for size in (n_e, n_e, n_c, n_e):
        scratch += [dma((size,)), dma((size,))]
    cube, rms = pl.pallas_call(
        functools.partial(kernel, n_e, n_c, skyc, comp),
        out_shape=(
            jax.ShapeDtypeStruct((fc, n_e, wl), f32),
            jax.ShapeDtypeStruct((fc, wl), f32),
        ),
        in_specs=[vmem, vmem, vmem, vmem, vmem, vmem, smem, smem, smem],
        out_specs=(vmem, vmem),
        scratch_shapes=scratch,
        compiler_params=pltpu.CompilerParams(
            collective_id=0, has_side_effects=True, vmem_limit_bytes=32 * 1024 * 1024
        ),
        name="extract",
    )(
        pixels.reshape(own, LANES),
        psf_proj,
        jnp.swapaxes(resolution, 0, 1),
        basis,
        fibre_slot.reshape(1, fc),
        band_shift.reshape(1, fc),
        sky_fibres,
        fibre_slot,
        band_shift,
    )
    return jnp.swapaxes(cube, 0, 1), rms


def solution(mesh):
    in_specs = (
        P("exp", "ccd", None, None),
        P("ccd", None, None),
        P("ccd", None, "exp"),
        P(),
        P(),
        P("ccd"),
        P("ccd"),
    )
    out_specs = (P(None, "ccd", "exp"), P("ccd", "exp"))
    body = functools.partial(shards, mesh.shape["exp"], mesh.shape["ccd"])
    return jax.shard_map(body, mesh=mesh, in_specs=in_specs, out_specs=out_specs, check_vma=False)
```

```python
import functools

import jax
import jax.numpy as jnp
from jax import lax
from jax.experimental import pallas as pl
from jax.experimental.pallas import tpu as pltpu
from jax.sharding import PartitionSpec as P

BPIX = 500
MARG = 20
ROWS = 4
BAND = 11
SHIFT = 3
SPAN = 540
LANES = 128
TAPS = BAND + 2 * SHIFT
HALO = MARG * ROWS
DEEP = SPAN * ROWS
SLOTS = 64
SKYROWS = 8
MESH = pl.DeviceIdType.MESH


def column_of(row, count):
    n = row.shape[1]
    sub = lax.broadcasted_iota(jnp.int32, (count, n), 0)
    lane = lax.broadcasted_iota(jnp.int32, (count, n), 1)
    return jnp.sum(jnp.where(sub == lane, row, 0), axis=1, keepdims=True)


def pieces_of(x):
    high = x.astype(jnp.bfloat16)
    rest = x - high.astype(jnp.float32)
    mid = rest.astype(jnp.bfloat16)
    low = (rest - mid.astype(jnp.float32)).astype(jnp.bfloat16)
    return high, mid, low


def kernel(
    n_e, n_c, skyc, comp,
    pix, psf, res, basis_ref, slot_row, shift_row, sky_s, slot_s, shift_s,
    out_ref, rms_ref,
    before, after, res2, bpad, bsh, stage, skysend, skyrecv, skyfull, slots, fluxr,
    fsend, frecv, grecv, csend, crecv, croll, outs,
    halo_ssem, halo_rsem, sky_ssem, sky_rsem, f_ssem, f_rsem,
    g_ssem, g_rsem, c_ssem, c_rsem,
):
    me = lax.axis_index("exp")
    mc = lax.axis_index("ccd")
    fc = res.shape[1]
    wl = res.shape[2]
    own = pix.shape[0]
    inner = before.shape[0] - HALO
    outer = after.shape[0] - HALO
    groups = LANES // wl
    tall = SLOTS // groups
    per = stage.shape[0]
    half = psf.shape[1]
    f32 = jnp.float32

    barrier = pltpu.get_barrier_semaphore()
    for d in range(1, n_e):
        pl.semaphore_signal(
            barrier, inc=1, device_id={"exp": lax.rem(me + d, n_e)}, device_id_type=MESH
        )
    for d in range(1, n_c):
        pl.semaphore_signal(
            barrier, inc=1, device_id={"ccd": lax.rem(mc + d, n_c)}, device_id_type=MESH
        )

    sky = [jnp.clip(sky_s[mc * skyc + i] - mc * fc, 0, fc - 1) for i in range(skyc)]

    stage[...] = jnp.zeros_like(stage)
    bpad[...] = jnp.zeros_like(bpad)
    bpad[0:comp, 0 : basis_ref.shape[1]] = basis_ref[...]
    for i in range(skyc):
        q, s = i // per, i % per
        for d in range(BAND):
            stage[s, d : d + 1, q * wl : (q + 1) * wl] = res[d, pl.ds(sky[i], 1), :]
    skysend[...] = stage[...].astype(jnp.bfloat16)

    pl.semaphore_wait(barrier, n_e - 1 + n_c - 1)

    def to_left():
        return pltpu.make_async_remote_copy(
            src_ref=pix.at[pl.ds(0, HALO)],
            dst_ref=after.at[pl.ds(outer, HALO)],
            send_sem=halo_ssem.at[0],
            recv_sem=halo_rsem.at[0],
            device_id={"ccd": lax.rem(mc + n_c - 1, n_c)},
            device_id_type=MESH,
        )

    def to_right():
        return pltpu.make_async_remote_copy(
            src_ref=pix.at[pl.ds(own - HALO, HALO)],
            dst_ref=before.at[pl.ds(0, HALO)],
            send_sem=halo_ssem.at[1],
            recv_sem=halo_rsem.at[1],
            device_id={"ccd": lax.rem(mc + 1, n_c)},
            device_id_type=MESH,
        )

    @pl.when(mc > 0)
    def _():
        to_left().start()

    @pl.when(mc < n_c - 1)
    def _():
        to_right().start()

    before[HALO:, :] = pix[0:inner, :]
    after[0:outer, :] = pix[own - outer :, :]

    @pl.when(mc == 0)
    def _():
        before[0:HALO, :] = jnp.zeros((HALO, LANES), before.dtype)

    @pl.when(mc == n_c - 1)
    def _():
        after[outer:, :] = jnp.zeros((HALO, LANES), after.dtype)

    def exchange(axis, size, mine, source, landing, ssem, rsem):
        sends, receives = [], []
        for d in range(1, size):
            there = lax.rem(mine + d, size)
            origin = lax.rem(mine + size - d, size)
            sends.append(
                pltpu.make_async_remote_copy(
                    src_ref=source(there), dst_ref=landing.at[mine],
                    send_sem=ssem.at[d], recv_sem=rsem.at[mine],
                    device_id={axis: there}, device_id_type=MESH,
                )
            )
            receives.append(
                pltpu.make_async_remote_copy(
                    src_ref=source(there), dst_ref=landing.at[origin],
                    send_sem=ssem.at[d], recv_sem=rsem.at[origin],
                    device_id={axis: there}, device_id_type=MESH,
                )
            )
        return sends, receives

    sky_out, sky_in = exchange(
        "exp", n_e, me, lambda there: skysend, skyrecv, sky_ssem, sky_rsem
    )
    for copy in sky_out:
        copy.start()
    skyrecv[me] = skysend[...]

    wide = bsh.shape[2]
    for e in range(TAPS):
        bsh[e] = bpad[:, e : e + wide]

    slot = column_of(slot_row[...], SLOTS) - mc * fc
    place = lax.broadcasted_iota(jnp.int32, (SLOTS, 1), 0)
    slot = jnp.where(place < fc, slot, -1000)
    sky_place = lax.broadcasted_iota(jnp.int32, (SKYROWS, 1), 0)
    sky_slot = jnp.full((SKYROWS, 1), -1000, jnp.int32)
    for i in range(skyc):
        sky_slot = jnp.where(sky_place == i, slot_s[sky[i]] - mc * fc, sky_slot)
    gap = slots.shape[0] // 2 - half

    def picker(rows):
        first = rows * ROWS + jnp.where(rows * ROWS >= half, gap, 0)
        lane = lax.broadcasted_iota(jnp.int32, (rows.shape[0], slots.shape[0]), 1)
        return jnp.concatenate(
            [jnp.where(lane == first + r, 1.0, 0.0) for r in range(ROWS)], axis=0
        ).astype(jnp.bfloat16)

    sky_pick, pick = picker(sky_slot), picker(slot)

    slots[...] = jnp.zeros_like(slots)

    def partial(block, lower, upper, window):
        weights = psf[block, :, lower:upper]
        wide_w = weights.astype(f32)
        wide_x = window.astype(f32)
        squares = (wide_w * wide_w).astype(jnp.bfloat16)
        pixvar = (0.25 + wide_x * wide_x).astype(jnp.bfloat16)
        flux = jnp.dot(weights, window, preferred_element_type=f32)
        var = jnp.dot(squares, pixvar, preferred_element_type=f32)
        return flux, var

    blocks = psf.shape[0]
    cuts = []
    for b in range(blocks):
        lower = before.shape[0] if b == 0 else 0
        upper = DEEP - after.shape[0] if b == blocks - 1 else DEEP
        cuts.append((lower, upper))
    main = []
    for b in range(blocks):
        start = b * BPIX * ROWS - HALO
        lower, upper = cuts[b]
        main.append(partial(b, lower, upper, pix[start + lower : start + upper, :]))

    @pl.when(mc < n_c - 1)
    def _():
        to_left().wait_recv()

    @pl.when(mc > 0)
    def _():
        to_right().wait_recv()

    pitch = slots.shape[0] // 2
    for b in range(blocks):
        flux, var = main[b]
        lower, upper = cuts[b]
        if lower > 0:
            more = partial(b, 0, lower, before[...])
            flux, var = flux + more[0], var + more[1]
        if upper < DEEP:
            more = partial(b, upper, DEEP, after[...])
            flux, var = flux + more[0], var + more[1]
        slots[b * pitch : b * pitch + half, 0:LANES] = flux
        slots[b * pitch : b * pitch + half, LANES:] = var

    pieces = pieces_of(slots[...])
    dot = functools.partial(jnp.dot, preferred_element_type=f32)

    def chosen(rows, lower, upper):
        parts = [dot(rows, x[:, lower:upper]) for x in pieces]
        return parts[0] + (parts[1] + parts[2])

    sky_rows = chosen(sky_pick, 0, 2 * LANES)

    for copy in sky_in:
        copy.wait_recv()
    for j in range(n_e):
        block = skyrecv[j].astype(f32)
        for i in range(skyc):
            q, s = i // per, i % per
            skyfull[i, :, j * wl : (j + 1) * wl] = block[s, :, q * wl : (q + 1) * wl]
    sub = lax.broadcasted_iota(jnp.int32, (16, wide), 0)
    sums = [jnp.zeros((16, LANES), f32) for _ in range(comp + 1)]
    for i in range(skyc):
        offset = jnp.clip(shift_s[sky[i]] + SHIFT, 0, 2 * SHIFT)
        model = jnp.zeros((16, wide), f32)
        for d in range(BAND):
            model = model + skyfull[i, d : d + 1, :] * bsh[offset + d]
        rows = [r * SKYROWS + i for r in range(ROWS)]
        flux = jnp.concatenate([sky_rows[x : x + 1, 0:LANES] for x in rows], axis=1)
        var = jnp.concatenate([sky_rows[x : x + 1, LANES:] for x in rows], axis=1)
        full = jnp.where(sub == comp, flux, model)
        weighted = full * (1.0 / var)
        for col in range(comp + 1):
            product = weighted * full[col : col + 1, :]
            for t in range(0, wide, LANES):
                sums[col] = sums[col] + product[:, t : t + LANES]
    lanes16 = lax.broadcasted_iota(jnp.int32, (16, LANES), 1)
    sub16 = lax.broadcasted_iota(jnp.int32, (16, LANES), 0)
    gram = jnp.zeros((16, LANES), f32)
    for col in range(comp + 1):
        gram = jnp.where(lanes16 == col, jnp.sum(sums[col], axis=1, keepdims=True), gram)
    grecv[mc] = gram
    g_out, g_in = exchange(
        "ccd", n_c, mc, lambda there: grecv.at[mc], grecv, g_ssem, g_rsem
    )
    for copy in g_out:
        copy.start()

    fluxr[...] = chosen(pick, 0, LANES)

    for j in range(n_e):
        r, off = j * wl // LANES, j * wl % LANES
        for q in range(groups):
            rows = pl.ds(r * SLOTS + q * tall, tall)
            fsend[j, :, q * wl : (q + 1) * wl] = fluxr[rows, off : off + wl]
    f_out, f_in = exchange(
        "exp", n_e, me, lambda there: fsend.at[there], frecv, f_ssem, f_rsem
    )
    for copy in f_out:
        copy.start()
    frecv[me] = fsend[me]

    planes = [res[d] for d in range(BAND)]
    shift = column_of(shift_row[...], fc) + SHIFT
    for step in (1, 2, 4):
        take = jnp.bitwise_and(shift, step) != 0
        length = min(len(planes) + step, TAPS)
        moved = []
        for e in range(length):
            here = planes[e] if e < len(planes) else jnp.zeros((fc, wl), f32)
            prior = planes[e - step] if e >= step else jnp.zeros((fc, wl), f32)
            moved.append(jnp.where(take, prior, here))
        planes = moved
    for e in range(TAPS):
        res2[e] = planes[e]

    for copy in g_in:
        copy.wait_recv()
    m = grecv[0]
    for c in range(1, n_c):
        m = m + grecv[c]
    for k in range(comp):
        row = m[k : k + 1, :] / m[k : k + 1, k : k + 1]
        m = jnp.where(sub16 == k, row, m - m[:, k : k + 1] * row)
    coeffs = jnp.where(sub16[:, 0:1] < comp, m[:, comp : comp + 1], 0.0)
    spectrum = jnp.sum(coeffs * bpad[...], axis=0, keepdims=True)
    for j in range(n_e):
        csend[j] = spectrum[:, j * wl : j * wl + LANES]
    c_out, c_in = exchange(
        "exp", n_e, me, lambda there: csend.at[there], crecv, c_ssem, c_rsem
    )
    for copy in c_out:
        copy.start()
    crecv[me] = csend[me]
    for copy in f_in:
        copy.wait_recv()
    for copy in c_in:
        copy.wait_recv()

    fitted = jnp.concatenate([crecv[e] for e in range(n_e)], axis=0)
    for e in range(TAPS):
        croll[e] = fitted if e == 0 else pltpu.roll(fitted, LANES - e, 1)

    for q in range(groups):
        base = q * tall
        count = min(tall, fc - base)
        if count <= 0:
            continue
        total = jnp.zeros((count, wl), f32)
        for e in range(n_e):
            glow = jnp.zeros((count, wl), f32)
            for t in range(TAPS):
                glow = glow + res2[t, base : base + count, :] * croll[t, e : e + 1, 0:wl]
            left = frecv[e, 0:count, q * wl : (q + 1) * wl] - glow
            outs[e, base : base + count, :] = left
            total = total + left
        mean = total / n_e
        square = jnp.zeros((count, wl), f32)
        for e in range(n_e):
            gone = outs[e, base : base + count, :] - mean
            square = square + gone * gone
        rms_ref[base : base + count, :] = jnp.sqrt(square / n_e + 1e-06)
    out_ref[...] = jnp.swapaxes(outs[...], 0, 1)

    @pl.when(mc > 0)
    def _():
        to_left().wait_send()

    @pl.when(mc < n_c - 1)
    def _():
        to_right().wait_send()

    for copy in sky_out + f_out + g_out + c_out:
        copy.wait_send()


def shards(n_e, n_c, pixels, psf_proj, resolution, basis, sky_fibres, fibre_slot, band_shift):
    fc, band, wl = resolution.shape
    comp, ext = basis.shape
    skyc = sky_fibres.shape[0] // n_c
    own = pixels.shape[1] * pixels.shape[2]
    wave = wl * n_e
    groups = LANES // wl
    per = -(-skyc // groups)
    half = psf_proj.shape[1]
    pitch = -(-half // 8) * 8
    f32, bf16 = jnp.float32, jnp.bfloat16
    vmem = pl.BlockSpec(memory_space=pltpu.VMEM)
    smem = pl.BlockSpec(memory_space=pltpu.SMEM)
    dma = pltpu.SemaphoreType.DMA
    scratch = [
        pltpu.VMEM((LANES, LANES), bf16),
        pltpu.VMEM((DEEP - (DEEP - HALO) // LANES * LANES, LANES), bf16),
        pltpu.VMEM((TAPS, fc, wl), f32),
        pltpu.VMEM((16, wave + LANES), f32),
        pltpu.VMEM((TAPS, 16, wave), f32),
        pltpu.VMEM((per, 16, LANES), f32),
        pltpu.VMEM((per, 16, LANES), bf16),
        pltpu.VMEM((n_e, per, 16, LANES), bf16),
        pltpu.VMEM((skyc, 16, wave), f32),
        pltpu.VMEM((2 * pitch, 2 * LANES), f32),
        pltpu.VMEM((ROWS * SLOTS, LANES), f32),
        pltpu.VMEM((n_e, SLOTS // groups, LANES), f32),
        pltpu.VMEM((n_e, SLOTS // groups, LANES), f32),
        pltpu.VMEM((n_c, 16, LANES), f32),
        pltpu.VMEM((n_e, 1, LANES), f32),
        pltpu.VMEM((n_e, 1, LANES), f32),
        pltpu.VMEM((TAPS, n_e, LANES), f32),
        pltpu.VMEM((n_e, fc, wl), f32),
        dma((2,)),
        dma((2,)),
    ]
    for size in (n_e, n_e, n_c, n_e):
        scratch += [dma((size,)), dma((size,))]
    cube, rms = pl.pallas_call(
        functools.partial(kernel, n_e, n_c, skyc, comp),
        out_shape=(
            jax.ShapeDtypeStruct((fc, n_e, wl), f32),
            jax.ShapeDtypeStruct((fc, wl), f32),
        ),
        in_specs=[vmem, vmem, vmem, vmem, vmem, vmem, smem, smem, smem],
        out_specs=(vmem, vmem),
        scratch_shapes=scratch,
        compiler_params=pltpu.CompilerParams(
            collective_id=0, has_side_effects=True, vmem_limit_bytes=32 * 1024 * 1024
        ),
        name="extract",
    )(
        pixels.reshape(own, LANES),
        psf_proj,
        jnp.swapaxes(resolution, 0, 1),
        basis,
        fibre_slot.reshape(1, fc),
        band_shift.reshape(1, fc),
        sky_fibres,
        fibre_slot,
        band_shift,
    )
    return jnp.swapaxes(cube, 0, 1), rms


def solution(mesh):
    in_specs = (
        P("exp", "ccd", None, None),
        P("ccd", None, None),
        P("ccd", None, "exp"),
        P(),
        P(),
        P("ccd"),
        P("ccd"),
    )
    out_specs = (P(None, "ccd", "exp"), P("ccd", "exp"))
    body = functools.partial(shards, mesh.shape["exp"], mesh.shape["ccd"])
    return jax.shard_map(body, mesh=mesh, in_specs=in_specs, out_specs=out_specs, check_vma=False)
```
